512 devices in a mesh: fsdp: 32 (over z, y_lo), head: 4 (over y_hi, core), rep: 4 (over x).
Axes of the slice: x: 4, y: 4 (y_hi: 2, y_lo: 2; y = y_hi * 2 + y_lo), z: 16, core: 2. Of those that a mesh axis runs over, the one named last changes fastest.
Arguments:
- query_up: bfloat16 [4, 1536, 64, 192], P('rep', 'fsdp', 'head'), may hold values from -1.796875 to 1.796875
- latent_up: bfloat16 [4, 512, 64, 256], P('rep', 'fsdp', 'head'), may hold values from -1.796875 to 1.796875
- latent_gain: float32 [4, 512], P('rep'), may hold values from 0.3 to 3
- server_heads: int32 [64], replicated, may hold values from 0 to 63, as said below
Outputs:
- absorbed: bfloat16 [4, 64, 1536, 512], P(None, 'head', 'fsdp')
The draws below stay inside these ranges and needn't reach their ends.
Inputs may be any that keep to these rules, and one draw needn't show every extreme that they name: `server_heads`: A permutation of the 64 heads. Slots o * 16 to (o + 1) * 16 - 1 belong to owner o; slot o * 16 + b * 4 + j, for j < 4, holds a head of block b, the heads b * 16 to (b + 1) * 16 - 1.
All inputs are finite; a program needn't handle non-finite values.
Results may differ from the reference program's by a relative error of at most 0.012.
Values may be sent and summed in bfloat16 or wider, within the bound.
A program may use at most 64 MiB of HBM per device.

```python
import math
import jax
import jax.numpy as jnp
from jax import lax

QR = 1536
KVR = 512
HEADS = 64
NOPE = 128
ROPE = 64
VDIM = 128
LAYERS = 4
HEADS_OWN = 16
HEADS_PAIR = 4
N_HEAD = 4


def draw_server_heads(key, part):
    key = jax.random.fold_in(key, 5)
    block_keys = jax.random.split(key, N_HEAD)
    orders = jax.vmap(lambda k: jax.random.permutation(k, HEADS_OWN))(block_keys)
    heads = orders.astype(jnp.int32) + (jnp.arange(N_HEAD, dtype=jnp.int32) * HEADS_OWN)[:, None]
    grouped = heads.reshape(N_HEAD, N_HEAD, HEADS_PAIR)
    return jnp.transpose(grouped, (1, 0, 2)).reshape(-1).astype(jnp.int32)


def shard_levels(rng, extent, cuts, smallest, largest):
    gain = 1.0
    for dim, parts in cuts:
        draws = jax.random.uniform(jax.random.fold_in(jax.random.fold_in(rng, 6), dim), (parts,), jnp.float32, smallest / len(cuts), largest / len(cuts))
        gain = gain * jnp.repeat(jnp.exp(draws), extent[dim] // parts).reshape((-1,) + (1,) * (len(extent) - 1 - dim))
    return gain


def noise(stream_key, extent, scale, bound, pieces=(), kind=jnp.bfloat16):
    drawn = scale * jax.random.normal(stream_key, extent, jnp.float32)
    if pieces:
        drawn = drawn * shard_levels(stream_key, extent, pieces, -0.22, 0.18)
    return jnp.clip(drawn, -bound, bound).astype(kind)


def setup_inputs(seed: int = 0) -> dict:
    arg_keys = jax.random.split(jax.random.key(seed), 5)
    query_up = noise(arg_keys[0], (LAYERS, QR, HEADS, NOPE + ROPE), 0.3, 1.796875, ((0, 4), (1, 32), (2, 4)))
    latent_up = noise(arg_keys[1], (LAYERS, KVR, HEADS, NOPE + VDIM), 0.3, 1.796875, ((0, 4), (1, 32), (2, 4)))
    latent_gain = jnp.clip(jnp.exp(math.log(3.0) - 2.3025851 * jax.random.uniform(arg_keys[2], (LAYERS, KVR), jnp.float32) ** shard_levels(arg_keys[2], (LAYERS, KVR), ((0, 4),), -0.2, 0.2)), 0.3, 3.0)
    server_heads = draw_server_heads(jax.random.fold_in(arg_keys[4], 71), 0)
    return {"query_up": query_up, "latent_up": latent_up, "latent_gain": latent_gain, "server_heads": server_heads}


def reference(query_up, latent_up, latent_gain, server_heads):
    query_nope = query_up[:, :, :, :NOPE]
    key_nope = latent_up[:, :, :, :NOPE]

    def one_layer(operands):
        query_layer, key_layer, gain_layer = operands
        chosen_query = jnp.take(query_layer, server_heads, axis=1).astype(jnp.float32)
        chosen_key = jnp.take(key_layer, server_heads, axis=1).astype(jnp.float32)
        product = jnp.einsum('rhd,chd->hrc', chosen_query, chosen_key)
        return (product * gain_layer[None, None, :]).astype(jnp.bfloat16)

    return lax.map(one_layer, (query_nope, key_nope, latent_gain))
```

```python
import jax
import jax.numpy as jnp
from jax import lax
from jax.experimental import pallas as pl
from jax.experimental.pallas import tpu as pltpu
from jax.sharding import PartitionSpec as P

MESH = pl.DeviceIdType.MESH
NOPE = 128
NZ = 16
LEGS = {1: (1,), 3: (1, 2), 6: (1, 2), -1: (-1,), -3: (-1,), -5: (-1, -2)}
FIRST = tuple(LEGS)
LAST = sum(len(v) for v in LEGS.values())
SPANS = sorted({abs(o) for o in FIRST} | {abs(s) for v in LEGS.values() for s in v})


def kernel(q_hbm, k_hbm, gain_ref, heads_ref, out_ref,
           q_in, k_in, q_f32, k_f32, q_send, k_send, q_all, k_all, prod,
           in_sem, ex_send, ex_recv, z_send, z_first, z_last, y_send, y_recv, x_send, x_recv, f_recv):
    f, b, x = lax.axis_index("fsdp"), lax.axis_index("head"), lax.axis_index("rep")
    z, yl, yh, c = f // 2, f % 2, b // 2, b % 2
    layers = lax.axis_size("rep")
    rows, cols = q_in.shape[0], k_in.shape[0]
    heads = q_in.shape[1]
    steps = heads // 2

    def device(zz=None, yy=None, hh=None, xx=None):
        return {
            "fsdp": (z if zz is None else zz) * 2 + (yl if yy is None else yy),
            "head": b if hh is None else hh,
            "rep": x if xx is None else xx,
        }

    def along_z(offset):
        return (z + offset + 2 * NZ) % NZ

    x_up, x_down = (x + 1) % layers, (x + layers - 1) % layers

    def owner(k):
        return (yh + k // 2) % 2 * 2 + (c + k % 2) % 2

    partners = [device(zz=along_z(s * v)) for v in SPANS for s in (1, -1)]
    partners += [device(xx=x_up), device(xx=x_down)]
    partners += [device(yy=(yl + e) % 2, hh=owner(k)) for k in range(4) for e in range(2) if (k, e) != (0, 0)]
    barrier = pltpu.get_barrier_semaphore()
    for p in partners:
        pl.semaphore_signal(barrier, inc=1, device_id=p, device_id_type=MESH)

    q_copy = pltpu.make_async_copy(q_hbm.at[0, :, :, pl.ds(0, NOPE)], q_in, in_sem.at[0])
    k_copy = pltpu.make_async_copy(k_hbm.at[0, :, :, pl.ds(0, NOPE)], k_in, in_sem.at[1])
    k_copy.start()
    q_copy.start()
    k_copy.wait()
    k_f32[...] = k_in[...].reshape(cols * heads, NOPE).astype(jnp.float32)
    my_rows = pl.ds(pl.multiple_of(z * 2 * cols + yl * cols, cols), cols)

    def head_of(t, half):
        return heads_ref[owner(t % 4) * heads + b * 4 + half * 2 + t // 4] % heads

    for t in range(steps):
        k_send[t] = k_f32[pl.ds(head_of(t, 1 - yl), cols, stride=heads), :].astype(jnp.bfloat16)
        k_all[t, my_rows, :] = k_f32[pl.ds(head_of(t, yl), cols, stride=heads), :].astype(jnp.bfloat16)
    q_copy.wait()
    q_f32[...] = q_in[...].reshape(rows * heads, NOPE).astype(jnp.float32)
    for t in range(steps):
        q_send[t] = q_f32[pl.ds(head_of(t, 1 - yl), rows, stride=heads), :].astype(jnp.bfloat16)
        q_all[t, yl] = q_f32[pl.ds(head_of(t, yl), rows, stride=heads), :].astype(jnp.bfloat16)

    pl.semaphore_wait(barrier, len(partners))

    mate = device(yy=1 - yl)

    def exchange(src, dst, i):
        return pltpu.make_async_remote_copy(
            src, dst, ex_send.at[i], ex_recv.at[i], device_id=mate, device_id_type=MESH)

    ex = [
        exchange(k_send.at[pl.ds(0, 1)], k_all.at[pl.ds(0, 1), my_rows], 0),
        exchange(k_send.at[pl.ds(1, steps - 1)], k_all.at[pl.ds(1, steps - 1), my_rows], 1),
        exchange(q_send, q_all.at[:, yl], 2),
    ]
    for e in ex:
        e.start()

    def slice_at(t, where):
        return k_all.at[t, pl.ds(pl.multiple_of(where * 2 * cols, 2 * cols), 2 * cols)]

    def z_copy(t, where, to, recv):
        ref = slice_at(t, where)
        return pltpu.make_async_remote_copy(
            ref, ref, z_send.at[t], recv, device_id=device(zz=to), device_id_type=MESH)

    def sign(t):
        return 1 - 2 * (t % 2)

    def first(t):
        for i, o in enumerate(FIRST):
            z_copy(t, z, along_z(sign(t) * o), z_first.at[t, i]).start()

    def relay(t):
        for i, o in enumerate(FIRST):
            origin = along_z(-sign(t) * o)
            z_copy(t, origin, z, z_first.at[t, i]).wait_recv()
            for s in LEGS[o]:
                z_copy(t, origin, along_z(sign(t) * s), z_last.at[t]).start()

    def y_copy(t, yy, hh, slot, half):
        return pltpu.make_async_remote_copy(
            prod.at[t, yy], out_ref.at[x, slot], y_send.at[t], y_recv.at[t, half],
            device_id=device(yy=yy, hh=hh), device_id_type=MESH)

    def multiply(t):
        pltpu.make_async_copy(
            k_all.at[t, pl.ds(0, LAST * 2 * cols)], k_all.at[t, pl.ds(0, LAST * 2 * cols)], z_last.at[t]).wait()
        product = lax.dot_general(
            q_all[t].reshape(2 * rows, NOPE), k_all[t], (((1,), (1,)), ((), ())),
            preferred_element_type=jnp.float32)
        prod[t] = (product * gain_ref[...]).astype(jnp.bfloat16).reshape(2, rows, product.shape[1])
        k = t % 4
        slot = b * 4 + yl * 2 + t // 4
        y_copy(t, 1 - yl, owner(k), slot, yl).start()

        @pl.when(k == 0)
        def _():
            out_ref[x, slot] = prod[t, yl]

        @pl.when(k != 0)
        def _():
            y_copy(t, yl, owner(k), slot, yl).start()

    def slot_of(t, half):
        return owner(t % 4) * 4 + half * 2 + t // 4

    def x_copy(layer, slot, to, t, recv):
        ref = out_ref.at[layer, slot]
        return pltpu.make_async_remote_copy(
            ref, ref, x_send.at[t], recv, device_id=device(xx=to), device_id_type=MESH)

    def spread(t):
        def both(half):
            slot = slot_of(t, half)
            x_copy(x, slot, x_up, t, x_recv.at[t, half, 0]).start()
            x_copy(x, slot, x_down, t, x_recv.at[t, half, 1]).start()

        @pl.when(t % 4 != 0)
        def _():
            y_copy(t, yl, b, 0, yl).wait_recv()

        both(yl)
        y_copy(t, yl, b, 0, 1 - yl).wait_recv()
        both(1 - yl)

    def forward(t):
        x_copy(x_down, slot_of(t, 0), x_up, t, x_recv.at[t, 0, 0]).wait_recv()
        x_copy(x_down, slot_of(t, 0), x_up, t, f_recv.at[t, 0]).start()
        x_copy(x_up, slot_of(t, 1), x_down, t, x_recv.at[t, 1, 1]).wait_recv()
        x_copy(x_up, slot_of(t, 1), x_down, t, f_recv.at[t, 1]).start()

    def collect(t):
        x_copy(x_up, slot_of(t, 0), x_up, t, x_recv.at[t, 0, 1]).wait_recv()
        x_copy(x_down, slot_of(t, 1), x_up, t, x_recv.at[t, 1, 0]).wait_recv()
        for half in range(2):
            x_copy((x + 2) % layers, slot_of(t, half), x_up, t, f_recv.at[t, half]).wait_recv()

    ex[0].wait_recv()
    first(0)
    ex[1].wait_recv()
    lax.fori_loop(1, steps, lambda t, _: (first(t), 0)[1], 0)
    ex[2].wait_recv()

    stages = ((relay, 0), (multiply, 3), (spread, 4), (forward, 6), (collect, 8))

    def turn(i, _):
        for stage, lag in stages:
            @pl.when((i >= lag) & (i < lag + steps))
            def _():
                stage(i - lag)
        return 0

    lax.fori_loop(0, steps + stages[-1][1], turn, 0)

    for e in ex:
        e.wait_send()

    def drain(t, _):
        pltpu.make_async_copy(
            k_all.at[t, pl.ds(0, (NZ - 1) * 2 * cols)], k_all.at[t, pl.ds(0, (NZ - 1) * 2 * cols)], z_send.at[t]).wait()
        y_copy(t, yl, b, 0, yl).wait_send()

        @pl.when(t % 4 != 0)
        def _():
            y_copy(t, yl, b, 0, yl).wait_send()

        pltpu.make_async_copy(
            out_ref.at[0, pl.ds(0, 6)], out_ref.at[0, pl.ds(0, 6)], x_send.at[t]).wait()
        return 0

    lax.fori_loop(0, steps, drain, 0)


def local(query_up, latent_up, latent_gain, server_heads):
    _, rows, heads, _ = query_up.shape
    cols = latent_up.shape[1]
    steps = heads // 2
    layers = lax.axis_size("rep")
    all_cols = latent_gain.shape[1]
    bf, dma = jnp.bfloat16, pltpu.SemaphoreType.DMA
    return pl.pallas_call(
        kernel,
        out_shape=jax.ShapeDtypeStruct((layers, heads, rows, all_cols), bf),
        in_specs=[
            pl.BlockSpec(memory_space=pl.ANY),
            pl.BlockSpec(memory_space=pl.ANY),
            pl.BlockSpec(memory_space=pltpu.VMEM),
            pl.BlockSpec(memory_space=pltpu.SMEM),
        ],
        out_specs=pl.BlockSpec(memory_space=pltpu.VMEM),
        scratch_shapes=[
            pltpu.VMEM((rows, heads, NOPE), bf),
            pltpu.VMEM((cols, heads, NOPE), bf),
            pltpu.VMEM((rows * heads, NOPE), jnp.float32),
            pltpu.VMEM((cols * heads, NOPE), jnp.float32),
            pltpu.VMEM((steps, rows, NOPE), bf),
            pltpu.VMEM((steps, cols, NOPE), bf),
            pltpu.VMEM((steps, 2, rows, NOPE), bf),
            pltpu.VMEM((steps, all_cols, NOPE), bf),
            pltpu.VMEM((steps, 2, rows, all_cols), bf),
            dma((2,)),
            dma((3,)),
            dma((3,)),
            dma((steps,)),
            dma((steps, len(FIRST))),
            dma((steps,)),
            dma((steps,)),
            dma((steps, 2)),
            dma((steps,)),
            dma((steps, 2, 2)),
            dma((steps, 2)),
        ],
        compiler_params=pltpu.CompilerParams(
            collective_id=0, has_side_effects=True, vmem_limit_bytes=48 << 20),
    )(query_up, latent_up, latent_gain, server_heads)


def solution(mesh):
    in_specs = (P("rep", "fsdp", "head", None), P("rep", "fsdp", "head", None), P("rep", None), P())
    out_specs = P(None, "head", "fsdp", None)
    return jax.shard_map(local, mesh=mesh, in_specs=in_specs, out_specs=out_specs, check_vma=False)
```

```python
import jax
import jax.numpy as jnp
from jax import lax
from jax.experimental import pallas as pl
from jax.experimental.pallas import tpu as pltpu
from jax.sharding import PartitionSpec as P

MESH = pl.DeviceIdType.MESH
NOPE = 128
NZ = 16
AHEAD = 3
LEGS = {1: (1,), 3: (1, 2), 6: (1, 2), -1: (-1,), -3: (-1,), -5: (-1, -2)}
FIRST = tuple(LEGS)
LAST = sum(len(v) for v in LEGS.values())
REACH = sorted({abs(o) for o in FIRST})
SPANS = sorted({abs(o) for o in FIRST} | {abs(s) for v in LEGS.values() for s in v})


def kernel(q_hbm, k_hbm, gain_hbm, heads_hbm, out_ref,
           gain_ref, heads_ref, q_in, k_in, q_f32, k_f32, q_send, k_send, q_all, k_all, prod,
           in_sem, ex_send, ex_recv, z_send, z_mate, z_first, z_last, y_send, y_recv, x_send, x_recv, f_recv):
    f, b, x = lax.axis_index("fsdp"), lax.axis_index("head"), lax.axis_index("rep")
    z, yl, yh, c = f // 2, f % 2, b // 2, b % 2
    layers = lax.axis_size("rep")
    rows, cols = q_in.shape[0], k_in.shape[0]
    heads = q_in.shape[1]
    steps = heads // 2

    def device(zz=None, yy=None, hh=None, xx=None):
        return {
            "fsdp": (z if zz is None else zz) * 2 + (yl if yy is None else yy),
            "head": b if hh is None else hh,
            "rep": x if xx is None else xx,
        }

    def along_z(offset):
        return (z + offset + 2 * NZ) % NZ

    x_up, x_down = (x + 1) % layers, (x + layers - 1) % layers

    def owner(k):
        return (yh + k // 2) % 2 * 2 + (c + k % 2) % 2

    partners = [device(zz=along_z(s * v)) for v in SPANS for s in (1, -1)]
    partners += [device(zz=along_z(s * v), yy=1 - yl) for v in REACH for s in (1, -1)]
    partners += [device(xx=x_up), device(xx=x_down)]
    partners += [device(yy=(yl + e) % 2, hh=owner(k)) for k in range(4) for e in range(2) if (k, e) != (0, 0)]
    barrier = pltpu.get_barrier_semaphore()
    for p in partners:
        pl.semaphore_signal(barrier, inc=1, device_id=p, device_id_type=MESH)

    copies = [
        pltpu.make_async_copy(heads_hbm, heads_ref, in_sem.at[0]),
        pltpu.make_async_copy(k_hbm.at[0, :, :, pl.ds(0, NOPE)], k_in, in_sem.at[1]),
        pltpu.make_async_copy(q_hbm.at[0, :, :, pl.ds(0, NOPE)], q_in, in_sem.at[2]),
        pltpu.make_async_copy(gain_hbm, gain_ref, in_sem.at[3]),
    ]
    for copy in copies:
        copy.start()
    copies[0].wait()
    copies[1].wait()
    k_f32[...] = k_in[...].reshape(cols * heads, NOPE).astype(jnp.float32)
    my_rows = pl.ds(pl.multiple_of(z * 2 * cols + yl * cols, cols), cols)

    def head_of(t, half):
        return heads_ref[owner(t % 4) * heads + b * 4 + half * 2 + t // 4] % heads

    for t in range(steps):
        k_send[t] = k_f32[pl.ds(head_of(t, 1 - yl), cols, stride=heads), :].astype(jnp.bfloat16)
        k_all[t, my_rows, :] = k_f32[pl.ds(head_of(t, yl), cols, stride=heads), :].astype(jnp.bfloat16)
    pl.semaphore_wait(barrier, len(partners))

    def slice_at(t, where):
        return k_all.at[t, pl.ds(pl.multiple_of(where * 2 * cols, 2 * cols), 2 * cols)]

    def z_copy(t, where, to, recv):
        ref = slice_at(t, where)
        return pltpu.make_async_remote_copy(
            ref, ref, z_send.at[t], recv, device_id=device(zz=to), device_id_type=MESH)

    mate = device(yy=1 - yl)

    def sign(t):
        return 1 - 2 * (t % 2)

    def first(t):
        for i, o in enumerate(FIRST):
            to = along_z(sign(t) * o)
            own = k_all.at[t, my_rows]
            for src, yy in ((own, yl), (k_send.at[t], 1 - yl)):
                pltpu.make_async_remote_copy(
                    src, own, z_send.at[t], z_first.at[t, i],
                    device_id=device(zz=to, yy=yy), device_id_type=MESH).start()
        pltpu.make_async_remote_copy(
            k_send.at[t], own, z_send.at[t], z_mate.at[t],
            device_id=mate, device_id_type=MESH).start()

    def relay(t):
        for i, o in enumerate(FIRST):
            origin = along_z(-sign(t) * o)
            z_copy(t, origin, z, z_first.at[t, i]).wait_recv()
            for s in LEGS[o]:
                z_copy(t, origin, along_z(sign(t) * s), z_last.at[t]).start()

        @pl.when(t + AHEAD < steps)
        def _():
            first(t + AHEAD)

    def y_copy(t, yy, hh, slot, half):
        return pltpu.make_async_remote_copy(
            prod.at[t, yy], out_ref.at[x, slot], y_send.at[t], y_recv.at[t, half],
            device_id=device(yy=yy, hh=hh), device_id_type=MESH)

    def multiply(t):
        pltpu.make_async_copy(
            k_all.at[t, pl.ds(0, LAST * 2 * cols)], k_all.at[t, pl.ds(0, LAST * 2 * cols)], z_last.at[t]).wait()
        pltpu.make_async_copy(k_all.at[t, my_rows], k_all.at[t, my_rows], z_mate.at[t]).wait()
        product = lax.dot_general(
            q_all[t].reshape(2 * rows, NOPE), k_all[t], (((1,), (1,)), ((), ())),
            preferred_element_type=jnp.float32)
        prod[t] = (product * gain_ref[...]).astype(jnp.bfloat16).reshape(2, rows, product.shape[1])
        k = t % 4
        slot = b * 4 + yl * 2 + t // 4
        y_copy(t, 1 - yl, owner(k), slot, yl).start()

        @pl.when(k == 0)
        def _():
            out_ref[x, slot] = prod[t, yl]

        @pl.when(k != 0)
        def _():
            y_copy(t, yl, owner(k), slot, yl).start()

    def slot_of(t, half):
        return owner(t % 4) * 4 + half * 2 + t // 4

    def x_copy(layer, slot, to, t, recv):
        ref = out_ref.at[layer, slot]
        return pltpu.make_async_remote_copy(
            ref, ref, x_send.at[t], recv, device_id=device(xx=to), device_id_type=MESH)

    def spread(t):
        def both(half):
            slot = slot_of(t, half)
            x_copy(x, slot, x_up, t, x_recv.at[t, half, 0]).start()
            x_copy(x, slot, x_down, t, x_recv.at[t, half, 1]).start()

        @pl.when(t % 4 != 0)
        def _():
            y_copy(t, yl, b, 0, yl).wait_recv()

        both(yl)
        y_copy(t, yl, b, 0, 1 - yl).wait_recv()
        both(1 - yl)

    def forward(t):
        x_copy(x_down, slot_of(t, 0), x_up, t, x_recv.at[t, 0, 0]).wait_recv()
        x_copy(x_down, slot_of(t, 0), x_up, t, f_recv.at[t, 0]).start()
        x_copy(x_up, slot_of(t, 1), x_down, t, x_recv.at[t, 1, 1]).wait_recv()
        x_copy(x_up, slot_of(t, 1), x_down, t, f_recv.at[t, 1]).start()

    def collect(t):
        x_copy(x_up, slot_of(t, 0), x_up, t, x_recv.at[t, 0, 1]).wait_recv()
        x_copy(x_down, slot_of(t, 1), x_up, t, x_recv.at[t, 1, 0]).wait_recv()
        for half in range(2):
            x_copy((x + 2) % layers, slot_of(t, half), x_up, t, f_recv.at[t, half]).wait_recv()

    for t in range(AHEAD):
        first(t)

    copies[2].wait()
    q_f32[...] = q_in[...].reshape(rows * heads, NOPE).astype(jnp.float32)
    for t in range(steps):
        q_send[t] = q_f32[pl.ds(head_of(t, 1 - yl), rows, stride=heads), :].astype(jnp.bfloat16)
    q_move = pltpu.make_async_remote_copy(
        q_send, q_all.at[:, yl], ex_send, ex_recv, device_id=mate, device_id_type=MESH)
    q_move.start()
    for t in range(steps):
        q_all[t, yl] = q_f32[pl.ds(head_of(t, yl), rows, stride=heads), :].astype(jnp.bfloat16)
    copies[3].wait()
    q_move.wait_recv()

    stages = ((relay, 0), (multiply, 1), (spread, 2), (forward, 4), (collect, 6))

    def turn(i, _):
        for stage, lag in stages:
            @pl.when((i >= lag) & (i < lag + steps))
            def _():
                stage(i - lag)
        return 0

    lax.fori_loop(0, steps + stages[-1][1], turn, 0)

    q_move.wait_send()

    def drain(t, _):
        sent = pl.ds(0, (2 * len(FIRST) + 1 + 2 * LAST) * cols)
        pltpu.make_async_copy(k_all.at[t, sent], k_all.at[t, sent], z_send.at[t]).wait()
        y_copy(t, yl, b, 0, yl).wait_send()

        @pl.when(t % 4 != 0)
        def _():
            y_copy(t, yl, b, 0, yl).wait_send()

        pltpu.make_async_copy(
            out_ref.at[0, pl.ds(0, 6)], out_ref.at[0, pl.ds(0, 6)], x_send.at[t]).wait()
        return 0

    lax.fori_loop(0, steps, drain, 0)


def local(query_up, latent_up, latent_gain, server_heads):
    _, rows, heads, _ = query_up.shape
    cols = latent_up.shape[1]
    steps = heads // 2
    layers = lax.axis_size("rep")
    all_cols = latent_gain.shape[1]
    bf, dma = jnp.bfloat16, pltpu.SemaphoreType.DMA
    return pl.pallas_call(
        kernel,
        out_shape=jax.ShapeDtypeStruct((layers, heads, rows, all_cols), bf),
        in_specs=[
            pl.BlockSpec(memory_space=pltpu.HBM)
        ] * 4,
        out_specs=pl.BlockSpec(memory_space=pltpu.VMEM),
        scratch_shapes=[
            pltpu.VMEM(latent_gain.shape, jnp.float32),
            pltpu.SMEM(server_heads.shape, jnp.int32),
            pltpu.VMEM((rows, heads, NOPE), bf),
            pltpu.VMEM((cols, heads, NOPE), bf),
            pltpu.VMEM((rows * heads, NOPE), jnp.float32),
            pltpu.VMEM((cols * heads, NOPE), jnp.float32),
            pltpu.VMEM((steps, rows, NOPE), bf),
            pltpu.VMEM((steps, cols, NOPE), bf),
            pltpu.VMEM((steps, 2, rows, NOPE), bf),
            pltpu.VMEM((steps, all_cols, NOPE), bf),
            pltpu.VMEM((steps, 2, rows, all_cols), bf),
            dma((4,)),
            dma,
            dma,
            dma((steps,)),
            dma((steps,)),
            dma((steps, len(FIRST))),
            dma((steps,)),
            dma((steps,)),
            dma((steps, 2)),
            dma((steps,)),
            dma((steps, 2, 2)),
            dma((steps, 2)),
        ],
        compiler_params=pltpu.CompilerParams(
            collective_id=0, has_side_effects=True, vmem_limit_bytes=48 << 20),
    )(*[pltpu.with_memory_space_constraint(a, pltpu.HBM) for a in (query_up, latent_up, latent_gain, server_heads)])


def solution(mesh):
    in_specs = (P("rep", "fsdp", "head", None), P("rep", "fsdp", "head", None), P("rep", None), P())
    out_specs = P(None, "head", "fsdp", None)
    return jax.shard_map(local, mesh=mesh, in_specs=in_specs, out_specs=out_specs, check_vma=False)
```

```python
import jax
import jax.numpy as jnp
from jax import lax
from jax.experimental import pallas as pl
from jax.experimental.pallas import tpu as pltpu
from jax.sharding import PartitionSpec as P

MESH = pl.DeviceIdType.MESH
NOPE = 128
NZ = 16
AHEAD = 2
ORDER = ("S0 F2 N0 S1", "N1 F3 T0 n0", "S2 N2 n1 T1", "R0 f0 S3 N3", "n2 T2 r0 f1", "R1 n3 f2 T3", "r1 R2 f3 g0", "r2 R3 g1 r3", "g2 g3")
LANES = 128
NEAR = (1, 2, -1, -2)
ROOTS = (3, -3)
SECOND = ((3, 1), (3, 3), (-3, -1), (-3, -3))
THIRD = ((4, (1,)), (6, (1, 2)), (-4, (-1,)), (-6, (-1,)))
N_THIRD = sum(len(v) for _, v in THIRD)


def kernel(q_hbm, k_hbm, gain_hbm, heads_hbm, out_ref,
           gain_ref, heads_ref, q_in, k_in, q_f32, k_f32, q_send, k_send, q_all, k_all, prod,
           in_sem, q_sent, q_recv, z_send, z_near, z_root, z_second, z_third,
           y_send, y_recv, x_send, x_recv, f_recv):
    f, b, x = lax.axis_index("fsdp"), lax.axis_index("head"), lax.axis_index("rep")
    z, yl, yh, c = f // 2, f % 2, b // 2, b % 2
    layers = lax.axis_size("rep")
    rows, cols = q_in.shape[0], k_in.shape[0]
    heads = q_in.shape[1]
    pairs, quarters = prod.shape[:2]
    cube = z // (NZ // quarters)

    def device(zz=None, yy=None, hh=None, xx=None):
        return {
            "fsdp": (z if zz is None else zz) * 2 + (yl if yy is None else yy),
            "head": b if hh is None else hh,
            "rep": x if xx is None else xx,
        }

    def along_z(offset):
        return (z + offset + 2 * NZ) % NZ

    x_up, x_down = (x + 1) % layers, (x + layers - 1) % layers

    def owner(k):
        return (yh + k // 2) % 2 * 2 + (c + k % 2) % 2

    partners = [device(zz=along_z(s), yy=yy) for s in NEAR + ROOTS for yy in (yl, 1 - yl)]
    partners += [device(xx=x_up), device(xx=x_down)]
    partners += [device(yy=(yl + e) % 2, hh=owner(k)) for k in range(4) for e in range(2) if (k, e) != (0, 0)]
    barrier = pltpu.get_barrier_semaphore()
    for p in partners:
        pl.semaphore_signal(barrier, inc=1, device_id=p, device_id_type=MESH)

    copies = [
        pltpu.make_async_copy(heads_hbm, heads_ref, in_sem.at[0]),
        pltpu.make_async_copy(k_hbm.at[0, :, :, pl.ds(0, NOPE)], k_in, in_sem.at[1]),
        pltpu.make_async_copy(q_hbm.at[0, :, :, pl.ds(0, NOPE)], q_in, in_sem.at[2]),
        pltpu.make_async_copy(gain_hbm, gain_ref, in_sem.at[3]),
    ]
    for copy in copies:
        copy.start()
    copies[0].wait()
    copies[1].wait()
    k_f32[...] = k_in[...].reshape(cols * heads, NOPE).astype(jnp.float32)
    my_rows = pl.ds(pl.multiple_of(z * 2 * cols + yl * cols, cols), cols)

    def head_of(k, j, half):
        return heads_ref[owner(k) * heads + b * 4 + half * 2 + j] % heads

    for k in range(pairs):
        for j in range(2):
            k_send[k, j] = k_f32[pl.ds(head_of(k, j, 1 - yl), cols, stride=heads), :].astype(jnp.bfloat16)
            k_all[k, j, my_rows, :] = k_f32[pl.ds(head_of(k, j, yl), cols, stride=heads), :].astype(jnp.bfloat16)
    pl.semaphore_wait(barrier, len(partners))

    mate = device(yy=1 - yl)

    def sign(k):
        return 1 - 2 * (k % 2)

    def first(k):
        own = k_all.at[k, :, my_rows]

        def send(src, to, sem):
            pltpu.make_async_remote_copy(
                src, own, z_send.at[k], sem, device_id=to, device_id_type=MESH).start()

        for i, o in enumerate(ROOTS):
            to = along_z(sign(k) * o)
            send(own, device(zz=to), z_root.at[k, i])
            send(k_send.at[k], device(zz=to, yy=1 - yl), z_root.at[k, i])
        for o in NEAR:
            to = along_z(sign(k) * o)
            send(own, device(zz=to), z_near.at[k])
            send(k_send.at[k], device(zz=to, yy=1 - yl), z_near.at[k])
        send(k_send.at[k], mate, z_near.at[k])

    def z_copy(k, origin, to, recv):
        ref = k_all.at[k, :, pl.ds(pl.multiple_of(origin * 2 * cols, 2 * cols), 2 * cols)]
        return pltpu.make_async_remote_copy(
            ref, ref, z_send.at[k], recv, device_id=device(zz=to), device_id_type=MESH)

    def arrived(k, n, sem):
        ref = k_all.at[k, :, pl.ds(0, n * cols)]
        pltpu.make_async_copy(ref, ref, sem).wait()

    def second(k):
        for i, o in enumerate(ROOTS):
            arrived(k, 2, z_root.at[k, i])
            for n, (root, s) in enumerate(SECOND):
                if root == o:
                    z_copy(k, along_z(-sign(k) * o), along_z(sign(k) * s), z_second.at[k, n]).start()

    def third(k):
        for n, (o, steps) in enumerate(THIRD):
            arrived(k, 2, z_second.at[k, n])
            for s in steps:
                z_copy(k, along_z(-sign(k) * o), along_z(sign(k) * s), z_third.at[k]).start()

    def lanes(i):
        return pl.ds(pl.multiple_of((cube + i) % quarters * LANES, LANES), LANES)

    def y_copy(k, i, yy, hh, slot, half):
        return pltpu.make_async_remote_copy(
            prod.at[k, i, yy], out_ref.at[x, pl.ds(slot, 2), :, lanes(i)], y_send.at[k], y_recv.at[k, i, half],
            device_id=device(yy=yy, hh=hh), device_id_type=MESH)

    def multiply(k, i):
        for j in range(2):
            product = lax.dot_general(
                q_all[k, j].reshape(2 * rows, NOPE), k_all[k, j, lanes(i), :], (((1,), (1,)), ((), ())),
                preferred_element_type=jnp.float32)
            product = (product * gain_ref[:, lanes(i)]).astype(jnp.bfloat16)
            prod[k, i, 0, j] = product[:rows]
            prod[k, i, 1, j] = product[rows:]
        slot = b * 4 + yl * 2
        y_copy(k, i, 1 - yl, owner(k), slot, yl).start()

        if k == 0:
            out_ref[x, pl.ds(slot, 2), :, lanes(i)] = prod[k, i, yl]
        else:
            y_copy(k, i, yl, owner(k), slot, yl).start()

    def multiply_near(k):
        arrived(k, 2 * len(NEAR) + 1, z_near.at[k])
        multiply(k, 0)

    def multiply_far(k):
        arrived(k, 2 * N_THIRD, z_third.at[k])
        for i in range(1, quarters):
            multiply(k, i)

    def x_copy(layer, k, i, half, to, recv):
        ref = out_ref.at[layer, pl.ds(owner(k) * 4 + half * 2, 2), :, lanes(i)]
        return pltpu.make_async_remote_copy(
            ref, ref, x_send.at[k], recv, device_id=device(xx=to), device_id_type=MESH)

    def spread(k, i):
        def both(half):
            x_copy(x, k, i, half, x_up, x_recv.at[k, i, half, 0]).start()
            x_copy(x, k, i, half, x_down, x_recv.at[k, i, half, 1]).start()

        if k != 0:
            y_copy(k, i, yl, b, 0, yl).wait_recv()
        both(yl)
        y_copy(k, i, yl, b, 0, 1 - yl).wait_recv()
        both(1 - yl)

    def forward(k, i):
        x_copy(x_down, k, i, 0, x_up, x_recv.at[k, i, 0, 0]).wait_recv()
        x_copy(x_down, k, i, 0, x_up, f_recv.at[k, i, 0]).start()
        x_copy(x_up, k, i, 1, x_down, x_recv.at[k, i, 1, 1]).wait_recv()
        x_copy(x_up, k, i, 1, x_down, f_recv.at[k, i, 1]).start()

    def collect(k):
        for i in range(quarters):
            x_copy(x_up, k, i, 0, x_up, x_recv.at[k, i, 0, 1]).wait_recv()
            x_copy(x_down, k, i, 1, x_up, x_recv.at[k, i, 1, 0]).wait_recv()
            for half in range(2):
                x_copy((x + 2) % layers, k, i, half, x_up, f_recv.at[k, i, half]).wait_recv()

    for k in range(AHEAD):
        first(k)

    copies[2].wait()
    q_f32[...] = q_in[...].reshape(rows * heads, NOPE).astype(jnp.float32)
    q_moves = []
    for k in range(pairs):
        for j in range(2):
            q_send[k, j] = q_f32[pl.ds(head_of(k, j, 1 - yl), rows, stride=heads), :].astype(jnp.bfloat16)
        if k in (0, pairs - 1):
            part = pl.ds(min(k, 1), max(k, 1))
            q_moves.append(pltpu.make_async_remote_copy(
                q_send.at[part], q_all.at[part, :, yl], q_sent.at[min(k, 1)], q_recv.at[min(k, 1)],
                device_id=mate, device_id_type=MESH))
            q_moves[-1].start()
    for k in range(pairs):
        for j in range(2):
            q_all[k, j, yl] = q_f32[pl.ds(head_of(k, j, yl), rows, stride=heads), :].astype(jnp.bfloat16)
    copies[3].wait()
    for move in q_moves:
        move.wait_recv()

    run = {
        "F": first, "S": second, "T": third, "N": multiply_near, "R": multiply_far, "n": lambda k: spread(k, 0),
        "f": lambda k: forward(k, 0),
        "r": lambda k: [spread(k, i) for i in range(1, quarters)],
        "g": lambda k: [forward(k, i) for i in range(1, quarters)],
    }
    for step in " ".join(ORDER).split():
        run[step[0]](int(step[1]))
    for k in range(pairs):
        collect(k)

    for move in q_moves:
        move.wait_send()

    for k in range(pairs):
        arrived(k, 2 * (len(NEAR) + len(ROOTS)) + 1 + 2 * (len(SECOND) + N_THIRD), z_send.at[k])
        for _ in range(1 if k == 0 else 2):
            pltpu.make_async_copy(prod.at[k, :, 0], prod.at[k, :, 0], y_send.at[k]).wait()
        sent = out_ref.at[0, pl.ds(0, 12)]
        pltpu.make_async_copy(sent, sent, x_send.at[k]).wait()


def local(query_up, latent_up, latent_gain, server_heads):
    _, rows, heads, _ = query_up.shape
    cols = latent_up.shape[1]
    pairs = heads // 4
    layers = lax.axis_size("rep")
    all_cols = latent_gain.shape[1]
    quarters = all_cols // LANES
    bf, dma = jnp.bfloat16, pltpu.SemaphoreType.DMA
    operands = [pltpu.with_memory_space_constraint(a, pltpu.HBM)
                for a in (query_up, latent_up, latent_gain, server_heads)]
    return pl.pallas_call(
        kernel,
        out_shape=jax.ShapeDtypeStruct((layers, heads, rows, all_cols), bf),
        in_specs=[pl.BlockSpec(memory_space=pltpu.HBM)] * 4,
        out_specs=pl.BlockSpec(memory_space=pltpu.VMEM),
        scratch_shapes=[
            pltpu.VMEM(latent_gain.shape, jnp.float32),
            pltpu.SMEM(server_heads.shape, jnp.int32),
            pltpu.VMEM((rows, heads, NOPE), bf),
            pltpu.VMEM((cols, heads, NOPE), bf),
            pltpu.VMEM((rows * heads, NOPE), jnp.float32),
            pltpu.VMEM((cols * heads, NOPE), jnp.float32),
            pltpu.VMEM((pairs, 2, rows, NOPE), bf),
            pltpu.VMEM((pairs, 2, cols, NOPE), bf),
            pltpu.VMEM((pairs, 2, 2, rows, NOPE), bf),
            pltpu.VMEM((pairs, 2, all_cols, NOPE), bf),
            pltpu.VMEM((pairs, quarters, 2, 2, rows, LANES), bf),
            dma((4,)),
            dma((2,)),
            dma((2,)),
            dma((pairs,)),
            dma((pairs,)),
            dma((pairs, len(ROOTS))),
            dma((pairs, len(SECOND))),
            dma((pairs,)),
            dma((pairs,)),
            dma((pairs, quarters, 2)),
            dma((pairs,)),
            dma((pairs, quarters, 2, 2)),
            dma((pairs, quarters, 2)),
        ],
        compiler_params=pltpu.CompilerParams(
            collective_id=0, has_side_effects=True, vmem_limit_bytes=48 << 20),
    )(*operands)


def solution(mesh):
    in_specs = (P("rep", "fsdp", "head", None), P("rep", "fsdp", "head", None), P("rep", None), P())
    out_specs = P(None, "head", "fsdp", None)
    return jax.shard_map(local, mesh=mesh, in_specs=in_specs, out_specs=out_specs, check_vma=False)
```

```python
import jax
import jax.numpy as jnp
from jax import lax
from jax.experimental import pallas as pl
from jax.experimental.pallas import tpu as pltpu
from jax.sharding import PartitionSpec as P

MESH = pl.DeviceIdType.MESH
NOPE = 128
NZ = 16
AHEAD = 3
ORDER = ("S0 N0 S1 N1", "n0 T0 M0 F3", "n1 S2 N2 p0", "T1 M1 R0 n2", "f0 S3 N3 p1", "r0 T2 M2 f1", "h0 n3 R1 T3", "M3 p2 f2 h1", "r1 g0 R2 p3", "f3 R3 r2 h2", "g1 r3 h3 g2", "g3")
LANES = 128
NEAR = (1, 2, -1, -2)
ROOTS = (3, -3)
SECOND = (1, 2, 3)
THIRD = ((6, (1, 2)), (-6, (-1,)))
N_MID = len(ROOTS) * (len(SECOND) - 1)
N_THIRD = sum(len(v) for _, v in THIRD)


def kernel(q_hbm, k_hbm, gain_hbm, heads_hbm, out_ref,
           gain_ref, heads_ref, q_in, k_in, q_f32, k_f32, q_send, k_send, q_all, k_all, prod,
           in_sem, q_sent, q_recv, z_send, z_near, z_root, z_second, z_mid, z_third,
           y_send, y_recv, x_send, x_recv, f_recv):
    f, b, x = lax.axis_index("fsdp"), lax.axis_index("head"), lax.axis_index("rep")
    z, yl, yh, c = f // 2, f % 2, b // 2, b % 2
    layers = lax.axis_size("rep")
    rows, cols = q_in.shape[0], k_in.shape[0]
    heads = q_in.shape[1]
    pairs, quarters = prod.shape[:2]
    cube = z // (NZ // quarters)

    def device(zz=None, yy=None, hh=None, xx=None):
        return {
            "fsdp": (z if zz is None else zz) * 2 + (yl if yy is None else yy),
            "head": b if hh is None else hh,
            "rep": x if xx is None else xx,
        }

    def along_z(offset):
        return (z + offset + 2 * NZ) % NZ

    x_up, x_down = (x + 1) % layers, (x + layers - 1) % layers

    def owner(k):
        return (yh + k // 2) % 2 * 2 + (c + k % 2) % 2

    partners = [device(zz=along_z(s), yy=yy) for s in NEAR + ROOTS for yy in (yl, 1 - yl)]
    partners += [device(xx=x_up), device(xx=x_down)]
    partners += [device(yy=(yl + e) % 2, hh=owner(k)) for k in range(4) for e in range(2) if (k, e) != (0, 0)]
    barrier = pltpu.get_barrier_semaphore()
    for p in partners:
        pl.semaphore_signal(barrier, inc=1, device_id=p, device_id_type=MESH)

    copies = [
        pltpu.make_async_copy(heads_hbm, heads_ref, in_sem.at[0]),
        pltpu.make_async_copy(k_hbm.at[0, :, :, pl.ds(0, NOPE)], k_in, in_sem.at[1]),
        pltpu.make_async_copy(q_hbm.at[0, :, :, pl.ds(0, NOPE)], q_in, in_sem.at[2]),
        pltpu.make_async_copy(gain_hbm, gain_ref, in_sem.at[3]),
    ]
    for copy in copies:
        copy.start()
    copies[0].wait()
    copies[1].wait()
    k_f32[...] = k_in[...].reshape(cols * heads, NOPE).astype(jnp.float32)
    my_rows = pl.ds(pl.multiple_of(z * 2 * cols + yl * cols, cols), cols)

    def head_of(k, j, half):
        return heads_ref[owner(k) * heads + b * 4 + half * 2 + j] % heads

    for k in range(pairs):
        for j in range(2):
            k_send[k, j] = k_f32[pl.ds(head_of(k, j, 1 - yl), cols, stride=heads), :].astype(jnp.bfloat16)
            k_all[k, j, my_rows, :] = k_f32[pl.ds(head_of(k, j, yl), cols, stride=heads), :].astype(jnp.bfloat16)
    pl.semaphore_wait(barrier, len(partners))

    mate = device(yy=1 - yl)

    def sign(k):
        return 1 - 2 * (k % 2)

    def first(k):
        own = k_all.at[k, :, my_rows]

        def send(src, to, sem):
            pltpu.make_async_remote_copy(
                src, own, z_send.at[k], sem, device_id=to, device_id_type=MESH).start()

        for i, o in enumerate(ROOTS):
            to = along_z(sign(k) * o)
            send(own, device(zz=to), z_root.at[k, i])
            send(k_send.at[k], device(zz=to, yy=1 - yl), z_root.at[k, i])
        for o in NEAR:
            to = along_z(sign(k) * o)
            send(own, device(zz=to), z_near.at[k])
            send(k_send.at[k], device(zz=to, yy=1 - yl), z_near.at[k])
        send(k_send.at[k], mate, z_near.at[k])

    def z_copy(k, origin, to, recv):
        ref = k_all.at[k, :, pl.ds(pl.multiple_of(origin * 2 * cols, 2 * cols), 2 * cols)]
        return pltpu.make_async_remote_copy(
            ref, ref, z_send.at[k], recv, device_id=device(zz=to), device_id_type=MESH)

    def arrived(k, n, sem):
        ref = k_all.at[k, :, pl.ds(0, n * cols)]
        pltpu.make_async_copy(ref, ref, sem).wait()

    def second(k):
        for i, o in enumerate(ROOTS):
            arrived(k, 2, z_root.at[k, i])
            for s in reversed(SECOND):
                sem = z_second.at[k, i] if s == SECOND[-1] else z_mid.at[k]
                z_copy(k, along_z(-sign(k) * o), along_z(sign(k) * s * (1 if o > 0 else -1)), sem).start()

    def third(k):
        for n, (o, steps) in enumerate(THIRD):
            arrived(k, 2, z_second.at[k, n])
            for s in steps:
                z_copy(k, along_z(-sign(k) * o), along_z(sign(k) * s), z_third.at[k]).start()

    def lanes(i):
        side = z % (NZ // quarters) // 2 * 2 - 1
        shift = (0, side, -side, 2)[i]
        return pl.ds(pl.multiple_of((cube + shift + quarters) % quarters * LANES, LANES), LANES)

    def y_copy(k, i, yy, hh, slot, half):
        return pltpu.make_async_remote_copy(
            prod.at[k, i, yy], out_ref.at[x, pl.ds(slot, 2), :, lanes(i)], y_send.at[k], y_recv.at[k, i, half],
            device_id=device(yy=yy, hh=hh), device_id_type=MESH)

    def multiply(k, i):
        for j in range(2):
            product = lax.dot_general(
                q_all[k, j].reshape(2 * rows, NOPE), k_all[k, j, lanes(i), :], (((1,), (1,)), ((), ())),
                preferred_element_type=jnp.float32)
            product = (product * gain_ref[:, lanes(i)]).astype(jnp.bfloat16)
            prod[k, i, 0, j] = product[:rows]
            prod[k, i, 1, j] = product[rows:]
        slot = b * 4 + yl * 2
        y_copy(k, i, 1 - yl, owner(k), slot, yl).start()

        if k == 0:
            out_ref[x, pl.ds(slot, 2), :, lanes(i)] = prod[k, i, yl]
        else:
            y_copy(k, i, yl, owner(k), slot, yl).start()

    def multiply_near(k):
        arrived(k, 2 * len(NEAR) + 1, z_near.at[k])
        multiply(k, 0)

    def multiply_mid(k):
        arrived(k, 2 * N_MID, z_mid.at[k])
        multiply(k, 1)

    def multiply_far(k):
        arrived(k, 2 * N_THIRD, z_third.at[k])
        for i in range(2, quarters):
            multiply(k, i)

    def x_copy(layer, k, i, half, to, recv):
        ref = out_ref.at[layer, pl.ds(owner(k) * 4 + half * 2, 2), :, lanes(i)]
        return pltpu.make_async_remote_copy(
            ref, ref, x_send.at[k], recv, device_id=device(xx=to), device_id_type=MESH)

    def spread(k, i):
        def both(half):
            x_copy(x, k, i, half, x_up, x_recv.at[k, i, half, 0]).start()
            x_copy(x, k, i, half, x_down, x_recv.at[k, i, half, 1]).start()

        if k != 0:
            y_copy(k, i, yl, b, 0, yl).wait_recv()
        both(yl)
        y_copy(k, i, yl, b, 0, 1 - yl).wait_recv()
        both(1 - yl)

    def forward(k, i):
        x_copy(x_down, k, i, 0, x_up, x_recv.at[k, i, 0, 0]).wait_recv()
        x_copy(x_down, k, i, 0, x_up, f_recv.at[k, i, 0]).start()
        x_copy(x_up, k, i, 1, x_down, x_recv.at[k, i, 1, 1]).wait_recv()
        x_copy(x_up, k, i, 1, x_down, f_recv.at[k, i, 1]).start()

    def collect(k):
        for i in range(quarters):
            x_copy(x_up, k, i, 0, x_up, x_recv.at[k, i, 0, 1]).wait_recv()
            x_copy(x_down, k, i, 1, x_up, x_recv.at[k, i, 1, 0]).wait_recv()
            for half in range(2):
                x_copy((x + 2) % layers, k, i, half, x_up, f_recv.at[k, i, half]).wait_recv()

    for k in range(AHEAD):
        first(k)

    copies[2].wait()
    q_f32[...] = q_in[...].reshape(rows * heads, NOPE).astype(jnp.float32)
    q_moves = []
    for k in range(pairs):
        for j in range(2):
            q_send[k, j] = q_f32[pl.ds(head_of(k, j, 1 - yl), rows, stride=heads), :].astype(jnp.bfloat16)
        if k in (0, pairs - 1):
            part = pl.ds(min(k, 1), max(k, 1))
            q_moves.append(pltpu.make_async_remote_copy(
                q_send.at[part], q_all.at[part, :, yl], q_sent.at[min(k, 1)], q_recv.at[min(k, 1)],
                device_id=mate, device_id_type=MESH))
            q_moves[-1].start()
    for k in range(pairs):
        for j in range(2):
            q_all[k, j, yl] = q_f32[pl.ds(head_of(k, j, yl), rows, stride=heads), :].astype(jnp.bfloat16)
    copies[3].wait()
    for move in q_moves:
        move.wait_recv()

    run = {
        "F": first, "S": second, "T": third, "N": multiply_near, "M": multiply_mid, "R": multiply_far,
        "n": lambda k: spread(k, 0), "p": lambda k: spread(k, 1),
        "r": lambda k: [spread(k, i) for i in range(2, quarters)],
        "f": lambda k: forward(k, 0), "h": lambda k: forward(k, 1),
        "g": lambda k: [forward(k, i) for i in range(2, quarters)],
    }
    for step in " ".join(ORDER).split():
        run[step[0]](int(step[1]))
    for k in range(pairs):
        collect(k)

    for move in q_moves:
        move.wait_send()

    for k in range(pairs):
        arrived(k, 2 * (len(NEAR) + len(ROOTS)) + 1 + 2 * (len(ROOTS) + N_MID + N_THIRD), z_send.at[k])
        for _ in range(1 if k == 0 else 2):
            pltpu.make_async_copy(prod.at[k, :, 0], prod.at[k, :, 0], y_send.at[k]).wait()
        sent = out_ref.at[0, pl.ds(0, 12)]
        pltpu.make_async_copy(sent, sent, x_send.at[k]).wait()


def local(query_up, latent_up, latent_gain, server_heads):
    _, rows, heads, _ = query_up.shape
    cols = latent_up.shape[1]
    pairs = heads // 4
    layers = lax.axis_size("rep")
    all_cols = latent_gain.shape[1]
    quarters = all_cols // LANES
    bf, dma = jnp.bfloat16, pltpu.SemaphoreType.DMA
    operands = [pltpu.with_memory_space_constraint(a, pltpu.HBM)
                for a in (query_up, latent_up, latent_gain, server_heads)]
    return pl.pallas_call(
        kernel,
        out_shape=jax.ShapeDtypeStruct((layers, heads, rows, all_cols), bf),
        in_specs=[pl.BlockSpec(memory_space=pltpu.HBM)] * 4,
        out_specs=pl.BlockSpec(memory_space=pltpu.VMEM),
        scratch_shapes=[
            pltpu.VMEM(latent_gain.shape, jnp.float32),
            pltpu.SMEM(server_heads.shape, jnp.int32),
            pltpu.VMEM((rows, heads, NOPE), bf),
            pltpu.VMEM((cols, heads, NOPE), bf),
            pltpu.VMEM((rows * heads, NOPE), jnp.float32),
            pltpu.VMEM((cols * heads, NOPE), jnp.float32),
            pltpu.VMEM((pairs, 2, rows, NOPE), bf),
            pltpu.VMEM((pairs, 2, cols, NOPE), bf),
            pltpu.VMEM((pairs, 2, 2, rows, NOPE), bf),
            pltpu.VMEM((pairs, 2, all_cols, NOPE), bf),
            pltpu.VMEM((pairs, quarters, 2, 2, rows, LANES), bf),
            dma((4,)),
            dma((2,)),
            dma((2,)),
            dma((pairs,)),
            dma((pairs,)),
            dma((pairs, len(ROOTS))),
            dma((pairs, len(ROOTS))),
            dma((pairs,)),
            dma((pairs,)),
            dma((pairs,)),
            dma((pairs, quarters, 2)),
            dma((pairs,)),
            dma((pairs, quarters, 2, 2)),
            dma((pairs, quarters, 2)),
        ],
        compiler_params=pltpu.CompilerParams(
            collective_id=0, has_side_effects=True, vmem_limit_bytes=48 << 20),
    )(*operands)


def solution(mesh):
    in_specs = (P("rep", "fsdp", "head", None), P("rep", "fsdp", "head", None), P("rep", None), P())
    out_specs = P(None, "head", "fsdp", None)
    return jax.shard_map(local, mesh=mesh, in_specs=in_specs, out_specs=out_specs, check_vma=False)
```

```python
import jax
import jax.numpy as jnp
from jax import lax
from jax.experimental import pallas as pl
from jax.experimental.pallas import tpu as pltpu
from jax.sharding import PartitionSpec as P

MESH = pl.DeviceIdType.MESH
NOPE = 128
NZ = 16
AHEAD = 3
ORDER = ("S0 N0 S1 N1", "n0 T0 M0 F3", "n1 S2 N2 T1", "M1 p0 R0 n2", "f0 S3 N3 p1", "r0 T2 M2 f1", "R1 h0 n3 T3", "M3 p2 f2 h1", "r1 R2 g0 p3", "f3 R3 r2 h2", "g1 r3 h3 g2", "g3")
LANES = 128
NEAR = (1, 2, -1, -2)
ROOTS = (3, -3)
SECOND = (1, 2, 3)
THIRD = ((6, (1, 2)), (-6, (-1,)))
N_MID = len(ROOTS) * (len(SECOND) - 1)
N_THIRD = sum(len(v) for _, v in THIRD)


def kernel(q_hbm, k_hbm, gain_hbm, heads_hbm, out_ref,
           gain_ref, heads_ref, q_in, k_in, q_f32, k_f32, q_send, k_send, q_all, k_all, prod,
           in_sem, q_sent, q_recv, z_send, z_near, z_root, z_second, z_mid, z_third,
           y_send, y_recv, x_send, x_recv, f_recv):
    f, b, x = lax.axis_index("fsdp"), lax.axis_index("head"), lax.axis_index("rep")
    z, yl, yh, c = f // 2, f % 2, b // 2, b % 2
    layers = lax.axis_size("rep")
    rows, cols = q_in.shape[0], k_in.shape[0]
    heads = q_in.shape[1]
    pairs, quarters = prod.shape[:2]
    cube = z // (NZ // quarters)

    def device(zz=None, yy=None, hh=None, xx=None):
        return {
            "fsdp": (z if zz is None else zz) * 2 + (yl if yy is None else yy),
            "head": b if hh is None else hh,
            "rep": x if xx is None else xx,
        }

    def along_z(offset):
        return (z + offset + 2 * NZ) % NZ

    x_up, x_down = (x + 1) % layers, (x + layers - 1) % layers

    def owner(k):
        return (yh + k // 2) % 2 * 2 + (c + k % 2) % 2

    partners = [device(zz=along_z(s), yy=yy) for s in NEAR + ROOTS for yy in (yl, 1 - yl)]
    partners += [device(xx=x_up), device(xx=x_down)]
    partners += [device(yy=(yl + e) % 2, hh=owner(k)) for k in range(4) for e in range(2) if (k, e) != (0, 0)]
    barrier = pltpu.get_barrier_semaphore()
    for p in partners:
        pl.semaphore_signal(barrier, inc=1, device_id=p, device_id_type=MESH)

    copies = [
        pltpu.make_async_copy(heads_hbm, heads_ref, in_sem.at[0]),
        pltpu.make_async_copy(k_hbm.at[0, :, :, pl.ds(0, NOPE)], k_in, in_sem.at[1]),
        pltpu.make_async_copy(q_hbm.at[0, :, :, pl.ds(0, NOPE)], q_in, in_sem.at[2]),
        pltpu.make_async_copy(gain_hbm, gain_ref, in_sem.at[3]),
    ]
    for copy in copies:
        copy.start()
    copies[0].wait()
    copies[1].wait()
    k_f32[...] = k_in[...].reshape(cols * heads, NOPE).astype(jnp.float32)
    my_rows = pl.ds(pl.multiple_of(z * 2 * cols + yl * cols, cols), cols)

    def head_of(k, j, half):
        return heads_ref[owner(k) * heads + b * 4 + half * 2 + j] % heads

    for k in range(pairs):
        for j in range(2):
            k_send[k, j] = k_f32[pl.ds(head_of(k, j, 1 - yl), cols, stride=heads), :].astype(jnp.bfloat16)
            k_all[k, j, my_rows, :] = k_f32[pl.ds(head_of(k, j, yl), cols, stride=heads), :].astype(jnp.bfloat16)
    pl.semaphore_wait(barrier, len(partners))

    mate = device(yy=1 - yl)

    def sign(k):
        return 1 - 2 * (k % 2)

    def first(k):
        own = k_all.at[k, :, my_rows]

        def send(src, to, sem):
            pltpu.make_async_remote_copy(
                src, own, z_send.at[k], sem, device_id=to, device_id_type=MESH).start()

        for i, o in enumerate(ROOTS):
            to = along_z(sign(k) * o)
            send(own, device(zz=to), z_root.at[k, i])
            send(k_send.at[k], device(zz=to, yy=1 - yl), z_root.at[k, i])
        for o in NEAR:
            to = along_z(sign(k) * o)
            send(own, device(zz=to), z_near.at[k])
            send(k_send.at[k], device(zz=to, yy=1 - yl), z_near.at[k])
        send(k_send.at[k], mate, z_near.at[k])

    def z_copy(k, origin, to, recv):
        ref = k_all.at[k, :, pl.ds(pl.multiple_of(origin * 2 * cols, 2 * cols), 2 * cols)]
        return pltpu.make_async_remote_copy(
            ref, ref, z_send.at[k], recv, device_id=device(zz=to), device_id_type=MESH)

    def arrived(k, n, sem):
        ref = k_all.at[k, :, pl.ds(0, n * cols)]
        pltpu.make_async_copy(ref, ref, sem).wait()

    def second(k):
        for i, o in enumerate(ROOTS):
            arrived(k, 2, z_root.at[k, i])
            for s in reversed(SECOND):
                sem = z_second.at[k, i] if s == SECOND[-1] else z_mid.at[k]
                z_copy(k, along_z(-sign(k) * o), along_z(sign(k) * s * (1 if o > 0 else -1)), sem).start()

    def third(k):
        for n, (o, steps) in enumerate(THIRD):
            arrived(k, 2, z_second.at[k, n])
            for s in steps:
                z_copy(k, along_z(-sign(k) * o), along_z(sign(k) * s), z_third.at[k]).start()

    def lanes(i):
        side = z % (NZ // quarters) // 2 * 2 - 1
        shift = (0, side, -side, 2)[i]
        return pl.ds(pl.multiple_of((cube + shift + quarters) % quarters * LANES, LANES), LANES)

    def y_copy(k, i, yy, hh, slot, half):
        return pltpu.make_async_remote_copy(
            prod.at[k, i, yy], out_ref.at[x, pl.ds(slot, 2), :, lanes(i)], y_send.at[k], y_recv.at[k, i, half],
            device_id=device(yy=yy, hh=hh), device_id_type=MESH)

    def multiply(k, i):
        for j in range(2):
            product = lax.dot_general(
                q_all[k, j].reshape(2 * rows, NOPE), k_all[k, j, lanes(i), :], (((1,), (1,)), ((), ())),
                preferred_element_type=jnp.float32)
            product = (product * gain_ref[:, lanes(i)]).astype(jnp.bfloat16)
            prod[k, i, 0, j] = product[:rows]
            prod[k, i, 1, j] = product[rows:]
        slot = b * 4 + yl * 2
        y_copy(k, i, 1 - yl, owner(k), slot, yl).start()

        if k == 0:
            out_ref[x, pl.ds(slot, 2), :, lanes(i)] = prod[k, i, yl]
        else:
            y_copy(k, i, yl, owner(k), slot, yl).start()

    def multiply_near(k):
        arrived(k, 2 * len(NEAR) + 1, z_near.at[k])
        multiply(k, 0)

    def multiply_mid(k):
        arrived(k, 2 * N_MID, z_mid.at[k])
        multiply(k, 1)

    def multiply_far(k):
        arrived(k, 2 * N_THIRD, z_third.at[k])
        for i in range(2, quarters):
            multiply(k, i)

    def x_copy(layer, k, i, half, to, recv):
        ref = out_ref.at[layer, pl.ds(owner(k) * 4 + half * 2, 2), :, lanes(i)]
        return pltpu.make_async_remote_copy(
            ref, ref, x_send.at[k], recv, device_id=device(xx=to), device_id_type=MESH)

    def spread(k, i):
        def both(half):
            x_copy(x, k, i, half, x_up, x_recv.at[k, i, half, 0]).start()
            x_copy(x, k, i, half, x_down, x_recv.at[k, i, half, 1]).start()

        if k != 0:
            y_copy(k, i, yl, b, 0, yl).wait_recv()
        both(yl)
        y_copy(k, i, yl, b, 0, 1 - yl).wait_recv()
        both(1 - yl)

    def forward(k, i):
        x_copy(x_down, k, i, 0, x_up, x_recv.at[k, i, 0, 0]).wait_recv()
        x_copy(x_down, k, i, 0, x_up, f_recv.at[k, i, 0]).start()
        x_copy(x_up, k, i, 1, x_down, x_recv.at[k, i, 1, 1]).wait_recv()
        x_copy(x_up, k, i, 1, x_down, f_recv.at[k, i, 1]).start()

    def collect(k):
        for i in range(quarters):
            x_copy(x_up, k, i, 0, x_up, x_recv.at[k, i, 0, 1]).wait_recv()
            x_copy(x_down, k, i, 1, x_up, x_recv.at[k, i, 1, 0]).wait_recv()
            for half in range(2):
                x_copy((x + 2) % layers, k, i, half, x_up, f_recv.at[k, i, half]).wait_recv()

    for k in range(AHEAD):
        first(k)

    copies[2].wait()
    q_f32[...] = q_in[...].reshape(rows * heads, NOPE).astype(jnp.float32)
    q_moves = []
    for k in range(pairs):
        for j in range(2):
            q_send[k, j] = q_f32[pl.ds(head_of(k, j, 1 - yl), rows, stride=heads), :].astype(jnp.bfloat16)
        if k in (0, pairs - 1):
            part = pl.ds(min(k, 1), max(k, 1))
            q_moves.append(pltpu.make_async_remote_copy(
                q_send.at[part], q_all.at[part, :, yl], q_sent.at[min(k, 1)], q_recv.at[min(k, 1)],
                device_id=mate, device_id_type=MESH))
            q_moves[-1].start()
    for k in range(pairs):
        for j in range(2):
            q_all[k, j, yl] = q_f32[pl.ds(head_of(k, j, yl), rows, stride=heads), :].astype(jnp.bfloat16)
    copies[3].wait()
    for move in q_moves:
        move.wait_recv()

    run = {
        "F": first, "S": second, "T": third, "N": multiply_near, "M": multiply_mid, "R": multiply_far,
        "n": lambda k: spread(k, 0), "p": lambda k: spread(k, 1),
        "r": lambda k: [spread(k, i) for i in range(2, quarters)],
        "f": lambda k: forward(k, 0), "h": lambda k: forward(k, 1),
        "g": lambda k: [forward(k, i) for i in range(2, quarters)],
    }
    for step in " ".join(ORDER).split():
        run[step[0]](int(step[1]))
    for k in range(pairs):
        collect(k)

    for move in q_moves:
        move.wait_send()

    for k in range(pairs):
        arrived(k, 2 * (len(NEAR) + len(ROOTS)) + 1 + 2 * (len(ROOTS) + N_MID + N_THIRD), z_send.at[k])
        for _ in range(1 if k == 0 else 2):
            pltpu.make_async_copy(prod.at[k, :, 0], prod.at[k, :, 0], y_send.at[k]).wait()
        sent = out_ref.at[0, pl.ds(0, 12)]
        pltpu.make_async_copy(sent, sent, x_send.at[k]).wait()


def local(query_up, latent_up, latent_gain, server_heads):
    _, rows, heads, _ = query_up.shape
    cols = latent_up.shape[1]
    pairs = heads // 4
    layers = lax.axis_size("rep")
    all_cols = latent_gain.shape[1]
    quarters = all_cols // LANES
    bf, dma = jnp.bfloat16, pltpu.SemaphoreType.DMA
    operands = [pltpu.with_memory_space_constraint(a, pltpu.HBM)
                for a in (query_up, latent_up, latent_gain, server_heads)]
    return pl.pallas_call(
        kernel,
        out_shape=jax.ShapeDtypeStruct((layers, heads, rows, all_cols), bf),
        in_specs=[pl.BlockSpec(memory_space=pltpu.HBM)] * 4,
        out_specs=pl.BlockSpec(memory_space=pltpu.VMEM),
        scratch_shapes=[
            pltpu.VMEM(latent_gain.shape, jnp.float32),
            pltpu.SMEM(server_heads.shape, jnp.int32),
            pltpu.VMEM((rows, heads, NOPE), bf),
            pltpu.VMEM((cols, heads, NOPE), bf),
            pltpu.VMEM((rows * heads, NOPE), jnp.float32),
            pltpu.VMEM((cols * heads, NOPE), jnp.float32),
            pltpu.VMEM((pairs, 2, rows, NOPE), bf),
            pltpu.VMEM((pairs, 2, cols, NOPE), bf),
            pltpu.VMEM((pairs, 2, 2, rows, NOPE), bf),
            pltpu.VMEM((pairs, 2, all_cols, NOPE), bf),
            pltpu.VMEM((pairs, quarters, 2, 2, rows, LANES), bf),
            dma((4,)),
            dma((2,)),
            dma((2,)),
            dma((pairs,)),
            dma((pairs,)),
            dma((pairs, len(ROOTS))),
            dma((pairs, len(ROOTS))),
            dma((pairs,)),
            dma((pairs,)),
            dma((pairs,)),
            dma((pairs, quarters, 2)),
            dma((pairs,)),
            dma((pairs, quarters, 2, 2)),
            dma((pairs, quarters, 2)),
        ],
        compiler_params=pltpu.CompilerParams(
            collective_id=0, has_side_effects=True, vmem_limit_bytes=48 << 20),
    )(*operands)


def solution(mesh):
    in_specs = (P("rep", "fsdp", "head", None), P("rep", "fsdp", "head", None), P("rep", None), P())
    out_specs = P(None, "head", "fsdp", None)
    return jax.shard_map(local, mesh=mesh, in_specs=in_specs, out_specs=out_specs, check_vma=False)
```
